32 devices in a mesh: groups: 2 (over y), ctx: 8 (over z, x), head: 2 (over core).
Axes of the slice: x: 2, y: 2, z: 4, core: 2. Of those that a mesh axis runs over, the one named last changes fastest.
Arguments:
- queries: bfloat16 [8192, 2048], P(('groups', 'ctx'), 'head'), parts along dimension 0, may hold values from -90 to 90
- keys: bfloat16 [8192, 2048], P(('groups', 'ctx'), 'head'), parts along dimension 0, may hold values from -7 to 7
- values: bfloat16 [8192, 2048], P(('groups', 'ctx'), 'head'), parts along dimension 0, may hold values from -6 to 6
- rates: float32 [4, 8192], P('head', ('groups', 'ctx')), parts along dimension 1, may hold values from 0.01 to 0.1
- windows: int32 [8], P(('groups', 'head')), parts along dimension 0, may hold values from 512 to 1024, as said below
- counts: int32 [16], P(('groups', 'ctx')), parts along dimension 0, may hold values from 128 to 512, as said below
- fast: bfloat16 [256, 4, 3, 512], P(None, 'head'), may hold values from -0.25 to 0.25
Outputs:
- mixed: bfloat16 [8192, 2048], P(('groups', 'ctx'), 'head'), parts along dimension 0
- new_fast: bfloat16 [512, 4, 3, 512], P(('groups', 'ctx'), 'head'), parts along dimension 0
The draws below stay inside these ranges and needn't reach their ends.
There are 2 independent parts, one for each index of `groups`. The reference program is written for one: setup_inputs(seed, part) draws one part's arguments, and reference() takes and returns one part's arrays. A program takes and returns all parts, laid end to end along the dimension named above; an argument that names none is the same for every part. Nothing has to cross between parts.
Inputs may be any that keep to these rules, and one draw needn't show every extreme that they name: `windows`: some head's window is exactly 1024. `counts`: some shard is full.
All inputs are finite; a program needn't handle non-finite values.
Results may differ from the reference program's by a relative error of at most 0.0065.
Values may be sent and summed in bfloat16 or wider, within the bound.
A program may use at most 128 MiB of HBM per device.

```python
import math
import jax
import jax.numpy as jnp
from jax import lax

HEADS = 4
HEAD_SIZE = 512
FH = 256
ATTENTION_SPAN = 1024
TOK_DEV = 512
LENGTH = 4096


def shared_keys(key):
    base = jax.random.normal(jax.random.fold_in(key, 11), (LENGTH, HEADS * HEAD_SIZE), jnp.float32)
    return jnp.clip(base, -6.0, 6.0)


def draw_keys(key, part):
    base = shared_keys(key)
    return base.astype(jnp.bfloat16)


def draw_queries(key, part):
    fresh = jax.random.normal(jax.random.fold_in(key, 23), (LENGTH, HEADS * HEAD_SIZE), jnp.float32)
    fresh = jnp.clip(fresh, -6.0, 6.0)
    return fresh.astype(jnp.bfloat16)


def draw_windows(key, part):
    chosen = jax.random.randint(jax.random.fold_in(key, 5), (), 0, HEADS)
    drawn = jax.random.randint(jax.random.fold_in(key, 6), (HEADS,), ATTENTION_SPAN // 2, ATTENTION_SPAN + 1)
    return drawn.at[chosen].set(ATTENTION_SPAN).astype(jnp.int32)


def draw_counts(key, part):
    shards = LENGTH // TOK_DEV
    chosen = jax.random.randint(jax.random.fold_in(key, 7), (), 0, shards)
    drawn = jax.random.randint(jax.random.fold_in(key, 8), (shards,), TOK_DEV // 4, TOK_DEV + 1)
    return drawn.at[chosen].set(TOK_DEV).astype(jnp.int32)


def steps_of(stream_key, shape, pieces, least, high):
    factor_of = 1.0
    for axis_at, blocks in pieces:
        heights = jax.random.uniform(jax.random.fold_in(jax.random.fold_in(stream_key, 6), axis_at), (blocks,), jnp.float32, least / len(pieces), high / len(pieces))
        factor_of = factor_of * jnp.repeat(jnp.exp(heights), shape[axis_at] // blocks).reshape((-1,) + (1,) * (len(shape) - 1 - axis_at))
    return factor_of


def gaussian(own_key, dims, deviation, reach, cuts=(), kind=jnp.bfloat16):
    result = deviation * jax.random.normal(own_key, dims, jnp.float32)
    if cuts:
        result = result * steps_of(own_key, dims, cuts, -0.22, 0.18)
    return jnp.clip(result, -reach, reach).astype(kind)


def setup_inputs(seed: int = 0, part: int = 0) -> dict:
    splits = jax.random.split(jax.random.key(seed), 8)
    part_keys = jax.random.split(jax.random.fold_in(splits[7], part), 8)
    queries = draw_queries(jax.random.fold_in(jax.random.fold_in(splits[7], part), 71), part)
    keys = draw_keys(jax.random.fold_in(jax.random.fold_in(splits[7], part), 71), part)
    values = gaussian(part_keys[2], (LENGTH, HEADS * HEAD_SIZE), 1.0, 6.0, ((0, 8), (1, 2)))
    rates = jnp.clip(jnp.exp(math.log(0.1) - 2.3025851 * jax.random.uniform(part_keys[3], (HEADS, LENGTH), jnp.float32) ** steps_of(part_keys[3], (HEADS, LENGTH), ((0, 2), (1, 8)), -0.2, 0.2)), 0.01, 0.1)
    windows = draw_windows(jax.random.fold_in(jax.random.fold_in(splits[7], part), 71), part)
    counts = draw_counts(jax.random.fold_in(jax.random.fold_in(splits[7], part), 71), part)
    fast = gaussian(splits[6], (FH, HEADS, 3, HEAD_SIZE), HEAD_SIZE ** -0.5, 0.25, ((1, 2),))
    return dict(queries=queries, keys=keys, values=values, rates=rates, windows=windows, counts=counts, fast=fast)


def reference(queries, keys, values, rates, windows, counts, fast):
    positions = jnp.arange(LENGTH, dtype=jnp.int32)
    shard = positions // TOK_DEV
    valid = positions - shard * TOK_DEV < counts[shard]
    validf = valid.astype(jnp.float32)
    block_number = math.gcd(LENGTH, 256)
    nblock = LENGTH // block_number
    results = []
    updated = []
    for h in range(HEADS):
        qh = queries[:, h * HEAD_SIZE:(h + 1) * HEAD_SIZE]
        kh = keys[:, h * HEAD_SIZE:(h + 1) * HEAD_SIZE]
        value_head = values[:, h * HEAD_SIZE:(h + 1) * HEAD_SIZE]
        w_one = fast[:, h, 0]
        w_down = fast[:, h, 1]
        w_three = fast[:, h, 2]
        h1 = jnp.dot(kh, w_one.T, preferred_element_type=jnp.float32)
        h3 = jnp.dot(kh, w_three.T, preferred_element_type=jnp.float32)
        dg = jnp.dot(value_head, w_down.T, preferred_element_type=jnp.float32)
        coef = (rates[h] * validf)[:, None]
        sig = jax.nn.sigmoid(h1)
        dh1 = (-coef * dg * h3 * sig * (1.0 + h1 * (1.0 - sig))).astype(jnp.bfloat16)
        dh3 = (-coef * dg * h1 * sig).astype(jnp.bfloat16)
        e_two = (-coef * h1 * sig * h3).astype(jnp.bfloat16)
        g_one = jnp.dot(dh1.T, kh, preferred_element_type=jnp.float32)
        g_two = jnp.dot(e_two.T, value_head, preferred_element_type=jnp.float32)
        g_three = jnp.dot(dh3.T, kh, preferred_element_type=jnp.float32)
        grads = jnp.stack([g_one, g_two, g_three], axis=1)
        upd = fast[:, h].astype(jnp.float32) - grads * LENGTH ** (-0.5)
        scale = lax.rsqrt(lax.optimization_barrier(jnp.mean(upd * upd, axis=-1, keepdims=True)) + 1e-06) * HEAD_SIZE ** (-0.5)
        newer = (upd * scale).astype(jnp.bfloat16)
        updated.append(newer)
        a_one = jnp.dot(qh, newer[:, 0].T, preferred_element_type=jnp.float32)
        a_three = jnp.dot(qh, newer[:, 2].T, preferred_element_type=jnp.float32)
        gated = (jax.nn.silu(a_one) * a_three).astype(jnp.bfloat16)
        ttt = jnp.dot(gated, newer[:, 1], preferred_element_type=jnp.float32) * FH ** (-0.5)
        kpad = jnp.concatenate([jnp.zeros((ATTENTION_SPAN, HEAD_SIZE), kh.dtype), kh], axis=0)
        value_padded = jnp.concatenate([jnp.zeros((ATTENTION_SPAN, HEAD_SIZE), value_head.dtype), value_head], axis=0)
        validpad = jnp.concatenate([jnp.zeros((ATTENTION_SPAN,), bool), valid], axis=0)
        limit = windows[h]

        def one_block(index):
            block_start = (index * block_number).astype(jnp.int32)
            q_block = lax.dynamic_slice_in_dim(qh, block_start, block_number, 0)
            k_block = lax.dynamic_slice_in_dim(kpad, block_start, block_number + ATTENTION_SPAN, 0)
            value_block = lax.dynamic_slice_in_dim(value_padded, block_start, block_number + ATTENTION_SPAN, 0)
            key_valid = lax.dynamic_slice_in_dim(validpad, block_start, block_number + ATTENTION_SPAN, 0)
            qpos = block_start + jnp.arange(block_number, dtype=jnp.int32)
            kpos = block_start - ATTENTION_SPAN + jnp.arange(block_number + ATTENTION_SPAN, dtype=jnp.int32)
            diff = qpos[:, None] - kpos[None, :]
            allowed = (diff >= 0) & (diff < limit) & (key_valid[None, :] | (diff == 0))
            scores = jnp.dot(q_block, k_block.T, preferred_element_type=jnp.float32) * HEAD_SIZE ** (-0.5)
            scores = jnp.where(allowed, scores, -1e+30)
            top = lax.optimization_barrier(jnp.max(scores, axis=1, keepdims=True))
            weights = jnp.where(allowed, jnp.exp(scores - top), 0.0)
            probs = (weights / lax.optimization_barrier(jnp.sum(weights, axis=1, keepdims=True))).astype(jnp.bfloat16)
            return jnp.dot(probs, value_block, preferred_element_type=jnp.float32)
        attn = lax.map(one_block, jnp.arange(nblock, dtype=jnp.int32)).reshape(LENGTH, HEAD_SIZE)
        results.append((validf[:, None] * (attn + ttt)).astype(jnp.bfloat16))
    mixed = jnp.concatenate(results, axis=1)
    new_fast = jnp.stack(updated, axis=1)
    return (mixed, new_fast)
```

```python
import functools
import jax
import jax.numpy as jnp
from jax import lax
from jax.experimental import pallas as pl
from jax.experimental.pallas import tpu as pltpu
from jax.sharding import PartitionSpec as P

MESH = pl.DeviceIdType.MESH
NT = (((1,), (1,)), ((), ()))
TN = (((0,), (0,)), ((), ()))
F32 = jnp.float32
BF16 = jnp.bfloat16


def dot(a, b, dims=None):
    if dims is None:
        return jnp.dot(a, b, preferred_element_type=F32)
    return lax.dot_general(a, b, dims, preferred_element_type=F32)


def kernel(n, cell, q_ref, k_ref, v_ref, rates_ref, win_ref, cnt_ref, fast_ref,
           mixed_ref, own_ref,
           r1, r2, cnt1, cnt2, gs, g32, rx, sz, rz, cross, newb, acc, mx, den,
           s1_sem, s2_sem, r1_sem, r2_sem, cs_sem, cr_sem,
           xs_sem, xr_sem, zs_sem, zr_sem, ks_sem, kr_sem,
           as_sem, ar_sem, fs_sem, fr_sem):
    heads, _, fh, dh = fast_ref.shape
    tok = q_ref.shape[0]
    length = tok * n
    me = lax.axis_index("ctx")
    rows = fh // cell
    nz = cell // 2
    cells = n // cell
    base = me // cell * cell
    pos = me % cell
    zc = pos // 2
    xc = pos % 2
    partner = base + 2 * zc + (1 - xc)
    tile = tok // 2

    barrier = pltpu.get_barrier_semaphore()

    @pl.loop(1, n)
    def _(i):
        pl.semaphore_signal(barrier, inc=1, device_id={"ctx": lax.rem(me + i, n)}, device_id_type=MESH)

    pl.semaphore_wait(barrier, n - 1)

    def rdma(src, dst, ssem, rsem, target):
        return pltpu.make_async_remote_copy(
            src_ref=src, dst_ref=dst, send_sem=ssem, recv_sem=rsem,
            device_id={"ctx": target}, device_id_type=MESH)

    kv_refs = (k_ref, v_ref)

    def own_kv(kv, h):
        return kv_refs[kv].at[:, h * dh:(h + 1) * dh]

    def to_two(kv, h):
        return rdma(own_kv(kv, h), r2.at[kv, h], s2_sem.at[kv, h], r2_sem.at[kv, h], me + 2)

    def to_one(kv, h):
        return rdma(own_kv(kv, h), r1.at[kv, h], s1_sem.at[kv, h], r1_sem.at[kv, h], me + 1)

    def relay(kv, h):
        return rdma(r2.at[kv, h], r1.at[kv, h], s1_sem.at[kv, h], r1_sem.at[kv, h], me - 1)

    def count_to(by):
        return rdma(cnt_ref, (cnt1, cnt2)[by - 1], cs_sem.at[by - 1], cr_sem.at[by - 1], me + by)

    even = me % 2 == 0
    relays = jnp.logical_and(me % 2 == 1, me >= 2)

    @pl.when(me + 1 < n)
    def _():
        count_to(1).start()

    @pl.when(me + 2 < n)
    def _():
        count_to(2).start()

    def send_kv(h):
        for kv in range(2):
            @pl.when(me + 2 < n)
            def _():
                to_two(kv, h).start()

            @pl.when(even)
            def _():
                to_one(kv, h).start()

    def relay_kv(h):
        for kv in range(2):
            @pl.when(relays)
            def _():
                to_two(kv, h).wait_recv()
                relay(kv, h).start()

    cnt_own = cnt_ref[0:1, 0:1]
    valid_col = lax.broadcasted_iota(jnp.int32, (tok, 1), 0) < cnt_own
    validf = valid_col.astype(F32)

    def x_copy(h):
        return rdma(gs.at[h, 1 - xc], rx.at[h], xs_sem.at[h], xr_sem.at[h], partner)

    def grads(h):
        cols = slice(h * dh, (h + 1) * dh)
        k = k_ref[:, cols]
        v = v_ref[:, cols]
        h1 = dot(k, fast_ref[h, 0], NT)
        dg = dot(v, fast_ref[h, 1], NT)
        h3 = dot(k, fast_ref[h, 2], NT)
        coef = -(rates_ref[:, h:h + 1] * validf)
        s = jax.nn.sigmoid(h1)
        cs = coef * s
        cdg = cs * dg
        dh1 = (cdg * h3 * (1.0 + h1 * (1.0 - s))).astype(BF16)
        dh3 = (cdg * h1).astype(BF16)
        e2 = (cs * h1 * h3).astype(BF16)
        for m, (left, right) in enumerate(((dh1, k), (e2, v), (dh3, k))):
            g = dot(left, right, TN)
            gb = g.astype(BF16)
            for d in range(cell):
                g32[h, d % 2, d // 2, m] = g[d * rows:(d + 1) * rows]
                gs[h, d % 2, d // 2, m] = gb[d * rows:(d + 1) * rows]
        x_copy(h).start()

    def z_target(i):
        return lax.rem(zc + i, nz)

    def z_send(h, i):
        t = z_target(i)
        return rdma(sz.at[h, t], rz.at[h, i - 1], zs_sem.at[h, i - 1], zr_sem.at[h, i - 1], base + 2 * t + xc)

    def pair_sum(h):
        x_copy(h).wait_recv()
        for z in range(nz):
            total = g32[h, xc, z] + rx[h, z].astype(F32)
            g32[h, xc, z] = total
            sz[h, z] = total.astype(BF16)
        for i in range(1, nz):
            z_send(h, i).start()

    def cross_send(h, i):
        slot = cells - 1 if cells > 1 else 0
        return rdma(cross.at[h, slot], cross.at[h, i - 1], ks_sem.at[h, i - 1], kr_sem.at[h, i - 1],
                    lax.rem(me + i * cell, n))

    def a_copy(h, i):
        block = newb.at[h, pos]
        return rdma(block, block, as_sem.at[h, i - 1], ar_sem.at[h, i - 1], base + 2 * z_target(i) + xc)

    def a_recv(h, i):
        src = lax.rem(zc + nz - i, nz)
        block = newb.at[h, 2 * src + xc]
        return rdma(block, block, as_sem.at[h, i - 1], ar_sem.at[h, i - 1], base + 2 * z_target(i) + xc)

    def f_copy(h, i):
        src = lax.rem(zc + nz - i, nz)
        block = newb.at[h, 2 * src + xc]
        return rdma(block, block, fs_sem.at[h, i], fr_sem.at[h, i], partner)

    def f_recv(h, i):
        src = lax.rem(zc + nz - i, nz)
        block = newb.at[h, 2 * src + 1 - xc]
        return rdma(block, block, fs_sem.at[h, i], fr_sem.at[h, i], partner)

    def norm(h):
        total = g32[h, xc, zc]
        for i in range(1, nz):
            z_send(h, i).wait_recv()
            total = total + rz[h, i - 1].astype(F32)
        if cells > 1:
            cross[h, cells - 1] = total.astype(BF16)
            g32[h, xc, zc] = total

            @pl.loop(1, cells)
            def _(i):
                cross_send(h, i).start()

            @pl.loop(1, cells)
            def _(i):
                cross_send(h, i).wait_recv()
                g32[h, xc, zc] = g32[h, xc, zc] + cross[h, i - 1].astype(F32)

            total = g32[h, xc, zc]
        old = fast_ref[h, :, pl.ds(pl.multiple_of(pos * rows, rows), rows), :].astype(F32)
        upd = old - total * length ** (-0.5)
        scale = lax.rsqrt(jnp.mean(upd * upd, axis=-1, keepdims=True) + 1e-06) * dh ** (-0.5)
        new = (upd * scale).astype(BF16)
        newb[h, pos] = new
        if cells == 1:
            own_ref[h, 0] = new
        for i in range(1, nz):
            a_copy(h, i).start()
        f_copy(h, 0).start()

    def forward(h):
        for i in range(1, nz):
            a_recv(h, i).wait_recv()
            f_copy(h, i).start()

    def attend(h, seg, t, k, v, j0, cnt, first):
        r = slice(t * tile, (t + 1) * tile)
        nk = k.shape[0]
        q = q_ref[r, h * dh:(h + 1) * dh]
        sc = dot(q, k, NT) * dh ** (-0.5)
        i = lax.broadcasted_iota(jnp.int32, (tile, nk), 0) + t * tile
        j = lax.broadcasted_iota(jnp.int32, (tile, nk), 1) + j0
        kv = (lax.broadcasted_iota(jnp.int32, (1, nk), 1) + j0) < cnt
        diff = i - j + seg * tok
        ok = (diff < win_ref[h]) & kv
        if seg == 0:
            ok = ((diff >= 0) & kv) | (diff == 0)
        sc = jnp.where(ok, sc, -1e30)
        top = jnp.max(sc, axis=1, keepdims=True)
        if first:
            p = jnp.exp(sc - top)
            mx[h, r] = top
            den[h, r] = jnp.sum(p, axis=1, keepdims=True)
            acc[h, r] = dot(p.astype(BF16), v)
        else:
            old = mx[h, r]
            top = jnp.maximum(old, top)
            p = jnp.exp(sc - top)
            fix = jnp.exp(old - top)
            mx[h, r] = top
            den[h, r] = den[h, r] * fix + jnp.sum(p, axis=1, keepdims=True)
            acc[h, r] = acc[h, r] * fix + dot(p.astype(BF16), v)

    def own_attend(h):
        cols = slice(h * dh, (h + 1) * dh)
        attend(h, 0, 0, k_ref[:tile, cols], v_ref[:tile, cols], 0, cnt_own, True)
        attend(h, 0, 1, k_ref[:, cols], v_ref[:, cols], 0, cnt_own, True)

    def two_attend(h):
        @pl.when(me >= 2)
        def _():
            @pl.when(even)
            def _():
                for kv in range(2):
                    to_two(kv, h).wait_recv()
            if h == 0:
                count_to(2).wait_recv()
            cnt = cnt2[0:1, 0:1]
            attend(h, 2, 0, r2[0, h], r2[1, h], 0, cnt, False)
            attend(h, 2, 1, r2[0, h, tile:], r2[1, h, tile:], tile, cnt, False)

    def one_attend(h):
        @pl.when(me >= 1)
        def _():
            for kv in range(2):
                to_one(kv, h).wait_recv()
            if h == 0:
                count_to(1).wait_recv()
            cnt = cnt1[0:1, 0:1]
            for t in range(2):
                attend(h, 1, t, r1[0, h], r1[1, h], 0, cnt, False)

    def apply(h):
        for i in range(nz):
            f_recv(h, i).wait_recv()
        w = [newb[h, :, m].reshape(fh, dh) for m in range(3)]
        for t in range(2):
            r = slice(t * tile, (t + 1) * tile)
            cols = slice(h * dh, (h + 1) * dh)
            q = q_ref[r, cols]
            a1 = dot(q, w[0], NT)
            a3 = dot(q, w[2], NT)
            ga = (a1 * jax.nn.sigmoid(a1) * a3).astype(BF16)
            ttt = dot(ga, w[1]) * fh ** (-0.5)
            attn = acc[h, r] / den[h, r]
            mixed_ref[r, cols] = jnp.where(valid_col[r], attn + ttt, 0.0).astype(BF16)

    send_kv(0)
    grads(0)
    grads(1)
    send_kv(1)
    own_attend(0)
    pair_sum(0)
    pair_sum(1)
    own_attend(1)
    norm(0)
    relay_kv(0)
    norm(1)
    forward(0)
    two_attend(0)
    forward(1)
    relay_kv(1)
    one_attend(0)
    two_attend(1)
    apply(0)
    one_attend(1)
    apply(1)

    for by in (1, 2):
        @pl.when(me + by < n)
        def _():
            count_to(by).wait_send()
    for h in range(heads):
        for kv in range(2):
            @pl.when(me + 2 < n)
            def _():
                to_two(kv, h).wait_send()

            @pl.when(even)
            def _():
                to_one(kv, h).wait_send()

            @pl.when(relays)
            def _():
                relay(kv, h).wait_send()
        x_copy(h).wait_send()
        for i in range(1, nz):
            z_send(h, i).wait_send()
            a_copy(h, i).wait_send()
        for i in range(nz):
            f_copy(h, i).wait_send()
        if cells > 1:
            @pl.loop(1, cells)
            def _(i):
                cross_send(h, i).wait_send()
            own_ref[h] = newb[h]


def on_device(n, queries, keys, values, rates, windows, counts, fast):
    tok, width = queries.shape
    fh, heads, mats, dh = fast.shape
    cell = min(n, 8)
    nz = cell // 2
    cells = n // cell
    rows = fh // cell
    rates_t = rates.T
    cnt = jnp.broadcast_to(counts[:, None], (8, 128))
    fast_t = jnp.transpose(fast, (1, 2, 0, 3))
    vmem = pl.BlockSpec(memory_space=pltpu.VMEM)
    smem = pl.BlockSpec(memory_space=pltpu.SMEM)
    blocks = 1 if cells == 1 else cell
    dma = pltpu.SemaphoreType.DMA
    near = max(nz - 1, 1)
    far = max(cells - 1, 1)
    mixed, own = pl.pallas_call(
        functools.partial(kernel, n, cell),
        out_shape=(
            jax.ShapeDtypeStruct((tok, width), BF16),
            jax.ShapeDtypeStruct((heads, blocks, mats, rows, dh), BF16),
        ),
        in_specs=[vmem, vmem, vmem, vmem, smem, vmem, vmem],
        out_specs=(vmem, vmem),
        scratch_shapes=[
            pltpu.VMEM((2, heads, tok, dh), BF16),
            pltpu.VMEM((2, heads, tok, dh), BF16),
            pltpu.VMEM((8, 128), jnp.int32),
            pltpu.VMEM((8, 128), jnp.int32),
            pltpu.VMEM((heads, 2, nz, mats, rows, dh), BF16),
            pltpu.VMEM((heads, 2, nz, mats, rows, dh), F32),
            pltpu.VMEM((heads, nz, mats, rows, dh), BF16),
            pltpu.VMEM((heads, nz, mats, rows, dh), BF16),
            pltpu.VMEM((heads, near, mats, rows, dh), BF16),
            pltpu.VMEM((heads, cells, mats, rows, dh) if cells > 1 else (1, 1, 1, 16, 128), BF16),
            pltpu.VMEM((heads, cell, mats, rows, dh), BF16),
            pltpu.VMEM((heads, tok, dh), F32),
            pltpu.VMEM((heads, tok, 1), F32),
            pltpu.VMEM((heads, tok, 1), F32),
            dma((2, heads)), dma((2, heads)), dma((2, heads)), dma((2, heads)),
            dma((2,)), dma((2,)),
            dma((heads,)), dma((heads,)),
            dma((heads, near)), dma((heads, near)),
            dma((heads, far)), dma((heads, far)),
            dma((heads, near)), dma((heads, near)),
            dma((heads, nz)), dma((heads, nz)),
        ],
        compiler_params=pltpu.CompilerParams(
            collective_id=0, has_side_effects=True, vmem_limit_bytes=50 * 2**20
        ),
    )(queries, keys, values, rates_t, windows, cnt, fast_t)
    if cells == 1:
        new_own = jnp.transpose(own[:, 0], (2, 0, 1, 3))
    else:
        full = jnp.transpose(own, (1, 3, 0, 2, 4)).reshape(fh, heads, mats, dh)
        share = fh // n
        new_own = lax.dynamic_slice_in_dim(full, lax.axis_index("ctx") * share, share, 0)
    return (mixed, new_own)


def solution(mesh):
    in_specs = (
        P(("groups", "ctx"), "head"),
        P(("groups", "ctx"), "head"),
        P(("groups", "ctx"), "head"),
        P("head", ("groups", "ctx")),
        P(("groups", "head")),
        P(("groups", "ctx")),
        P(None, "head", None, None),
    )
    out_specs = (P(("groups", "ctx"), "head"), P(("groups", "ctx"), "head", None, None))
    return jax.shard_map(
        functools.partial(on_device, mesh.shape["ctx"]),
        mesh=mesh, in_specs=in_specs, out_specs=out_specs, check_vma=False
    )
```

```python
import functools
import jax
import jax.numpy as jnp
from jax import lax
from jax.experimental import pallas as pl
from jax.experimental.pallas import tpu as pltpu
from jax.sharding import PartitionSpec as P

MESH = pl.DeviceIdType.MESH
NT = (((1,), (1,)), ((), ()))
TN = (((0,), (0,)), ((), ()))
F32 = jnp.float32
BF16 = jnp.bfloat16


def dot(a, b, dims=None):
    if dims is None:
        return jnp.dot(a, b, preferred_element_type=F32)
    return lax.dot_general(a, b, dims, preferred_element_type=F32)


def kernel(n, cell, q_ref, k_ref, v_ref, meta_ref, win_ref, fast_ref,
           mixed_ref, own_ref,
           kvq, prev, metas, gs, g32, rz, cross, newb, xbuf, acc, mx, den, ttt, outs, outr,
           x_s, x_r, d_s, d_r, y_s, y_r, m_s, m_r, z_s, z_r, c_s, c_r, a_s, a_r, n_s, n_r, o_s, o_r):
    _, _, fh, dh = fast_ref.shape
    tok = q_ref.shape[0]
    length = tok * n
    me = lax.axis_index("ctx")
    nz = cell // 2
    cells = n // cell
    rows = fh // nz
    half = rows // 2
    base = me // cell * cell
    zc = me % cell // 2
    xc = me % 2
    oc = 1 - xc
    partner = me + 1 - 2 * xc
    tile = tok // 2
    has_prev = me >= 2
    has_next = me + 2 < n

    barrier = pltpu.get_barrier_semaphore()

    @pl.loop(1, n)
    def _(i):
        pl.semaphore_signal(barrier, inc=1, device_id={"ctx": lax.rem(me + i, n)}, device_id_type=MESH)

    pl.semaphore_wait(barrier, n - 1)

    def rdma(src, dst, ssem, rsem, target):
        return pltpu.make_async_remote_copy(
            src_ref=src, dst_ref=dst, send_sem=ssem, recv_sem=rsem,
            device_id={"ctx": target}, device_id_type=MESH)

    refs = (k_ref, v_ref, q_ref)
    mine = pl.ds(pl.multiple_of(xc * dh, dh), dh)
    other = pl.ds(pl.multiple_of(oc * dh, dh), dh)

    def swap(i):
        return rdma(refs[i].at[:, other], kvq.at[i, xc], x_s.at[i], x_r.at[i], partner)

    def direct(i):
        return rdma(refs[i].at[:, mine], prev.at[i, xc], d_s.at[i], d_r.at[i], me + 2)

    def relay(i):
        return rdma(kvq.at[i, oc], prev.at[i, oc], y_s.at[i], y_r.at[i], me + 2)

    def meta_pair():
        return rdma(meta_ref, metas.at[2], m_s.at[0], m_r.at[0], partner)

    def meta_next(same):
        return rdma(meta_ref, metas.at[xc], m_s.at[2 - same], m_r.at[2 - same], (me if same else partner) + 2)

    def z_target(i):
        return base + 2 * lax.rem(zc + i, nz) + xc

    def z_send(i):
        return rdma(gs.at[lax.rem(zc + i, nz)], rz.at[i - 1], z_s.at[i - 1], z_r.at[i - 1], z_target(i))

    def cross_send(i):
        return rdma(cross.at[cells - 1], cross.at[i - 1], c_s.at[i - 1], c_r.at[i - 1], lax.rem(me + i * cell, n))

    def a_send(i):
        return rdma(newb.at[zc], newb.at[zc], a_s.at[i - 1], a_r.at[i - 1], z_target(i))

    def a_recv(i):
        block = newb.at[lax.rem(zc + nz - i, nz)]
        return rdma(block, block, a_s.at[i - 1], a_r.at[i - 1], z_target(i))

    def new_swap():
        if cells == 1:
            part = newb.at[zc, :, pl.ds(pl.multiple_of(oc * half, half), half)]
        else:
            part = newb
        return rdma(part, xbuf, n_s.at[0], n_r.at[0], partner)

    def out_send(t):
        r = pl.ds(t * tile, tile)
        return rdma(outs.at[r], outr.at[r], o_s.at[t], o_r.at[t], partner)

    meta_pair().start()

    @pl.when(has_next)
    def _():
        meta_next(1).start()
        meta_next(0).start()

    for i in range(2):
        swap(i).start()

        @pl.when(has_next)
        def _():
            direct(i).start()
    swap(2).start()

    for i in range(3):
        kvq[i, xc] = refs[i][:, mine]

    window = win_ref[xc]

    def count_of(m):
        return m[2:3, 0:1].astype(jnp.int32)

    def valid_of(cnt):
        return lax.broadcasted_iota(jnp.int32, (tok, 1), 0) < cnt

    cnt_own = count_of(meta_ref)

    def grads(s, meta, first):
        k = kvq[0, s]
        v = kvq[1, s]
        h1 = dot(k, fast_ref[xc, 0], NT)
        dg = dot(v, fast_ref[xc, 1], NT)
        h3 = dot(k, fast_ref[xc, 2], NT)
        turned = jnp.transpose(meta[...])
        rate = jnp.where(xc == 0, turned[:, 0:1], turned[:, 1:2])
        coef = -(rate * valid_of(count_of(meta)).astype(F32))
        sg = jax.nn.sigmoid(h1)
        cs = coef * sg
        cdg = cs * dg
        dh1 = (cdg * h3 * (1.0 + h1 * (1.0 - sg))).astype(BF16)
        dh3 = (cdg * h1).astype(BF16)
        e2 = (cs * h1 * h3).astype(BF16)
        for m, (left, right) in enumerate(((dh1, k), (e2, v), (dh3, k))):
            g = dot(left, right, TN)
            for z in range(nz):
                part = g[z * rows:(z + 1) * rows]
                if first:
                    g32[z, m] = part
                else:
                    part = part + g32[z, m]
                    g32[z, m] = part
                    gs[z, m] = part.astype(BF16)

    def norm():
        total = g32[zc]
        for i in range(1, nz):
            z_send(i).wait_recv()
            total = total + rz[i - 1].astype(F32)
        if cells > 1:
            cross[cells - 1] = total.astype(BF16)
            g32[zc] = total

            @pl.loop(1, cells)
            def _(i):
                cross_send(i).start()

            @pl.loop(1, cells)
            def _(i):
                cross_send(i).wait_recv()
                g32[zc] = g32[zc] + cross[i - 1].astype(F32)

            total = g32[zc]
        old = fast_ref[xc, :, pl.ds(pl.multiple_of(zc * rows, rows), rows), :].astype(F32)
        upd = old - total * length ** (-0.5)
        scale = lax.rsqrt(jnp.mean(upd * upd, axis=-1, keepdims=True) + 1e-06) * dh ** (-0.5)
        newb[zc] = (upd * scale).astype(BF16)
        for i in range(1, nz):
            a_send(i).start()
        if cells == 1:
            new_swap().start()
            own_ref[xc] = newb[zc, :, pl.ds(pl.multiple_of(xc * half, half), half)]

    def attend(qs, seg, t, k, v, j0, cnt):
        r = slice(t * tile, (t + 1) * tile)
        nk = k.shape[0]
        sc = dot(kvq[2, qs, r], k, NT) * dh ** (-0.5)
        i = lax.broadcasted_iota(jnp.int32, (tile, nk), 0) + t * tile
        j = lax.broadcasted_iota(jnp.int32, (tile, nk), 1) + j0
        kv = (lax.broadcasted_iota(jnp.int32, (1, nk), 1) + j0) < cnt
        diff = i - j + seg * tok
        if seg == 0:
            ok = ((diff >= 0) & kv) | (diff == 0)
        else:
            ok = (diff < window) & kv
        sc = jnp.where(ok, sc, -1e30)
        top = jnp.max(sc, axis=1, keepdims=True)
        if seg == 0:
            p = jnp.exp(sc - top)
            mx[qs, r] = top
            den[qs, r] = jnp.sum(p, axis=1, keepdims=True)
            acc[qs, r] = dot(p.astype(BF16), v)
        else:
            old = mx[qs, r]
            top = jnp.maximum(old, top)
            p = jnp.exp(sc - top)
            fix = jnp.exp(old - top)
            mx[qs, r] = top
            den[qs, r] = den[qs, r] * fix + jnp.sum(p, axis=1, keepdims=True)
            acc[qs, r] = acc[qs, r] * fix + dot(p.astype(BF16), v)

    def causal(s, cnt):
        attend(s, 0, 0, kvq[0, s, :tile], kvq[1, s, :tile], 0, cnt)
        attend(s, 0, 1, kvq[0, s], kvq[1, s], 0, cnt)

    def full(qs, k, v, cnt):
        for t in range(2):
            attend(qs, 1, t, k, v, 0, cnt)

    def far(qs, ks, cnt):
        attend(qs, 2, 0, prev[0, ks], prev[1, ks], 0, cnt)
        attend(qs, 2, 1, prev[0, ks, tile:], prev[1, ks, tile:], tile, cnt)

    def prev_step(ks, arrived):
        @pl.when(jnp.logical_and(has_prev, arrived))
        def _():
            cnt = count_of(metas[ks])
            far(ks, ks, cnt)
            if ks == 1:
                full(0, prev[0, 1], prev[1, 1], cnt)

    def apply(s):
        w = [newb[:, m].reshape(fh, dh) for m in range(3)]
        for t in range(2):
            r = slice(t * tile, (t + 1) * tile)
            q = kvq[2, s, r]
            a1 = dot(q, w[0], NT)
            a3 = dot(q, w[2], NT)
            ga = (a1 * jax.nn.sigmoid(a1) * a3).astype(BF16)
            ttt[s, r] = dot(ga, w[1]) * fh ** (-0.5)

    def result(s, cnt, t):
        r = slice(t * tile, (t + 1) * tile)
        return jnp.where(valid_of(cnt)[r], acc[s, r] / den[s, r] + ttt[s, r], 0.0).astype(BF16)

    grads(xc, meta_ref, True)
    causal(xc, cnt_own)
    meta_pair().wait_recv()
    cnt_pair = count_of(metas[2])
    for i in range(2):
        swap(i).wait_recv()
    grads(oc, metas.at[2], False)
    for i in range(1, nz):
        z_send(i).start()

    @pl.when(has_next)
    def _():
        for i in range(2):
            relay(i).start()

    swap(2).wait_recv()
    causal(oc, cnt_pair)
    full(1, kvq[0, 0], kvq[1, 0], jnp.where(xc == 0, cnt_own, cnt_pair))
    norm()

    @pl.when(has_prev)
    def _():
        meta_next(1).wait_recv()
        meta_next(0).wait_recv()
        for i in range(2):
            direct(i).wait_recv()

    prev_step(0, xc == 0)
    prev_step(1, xc == 1)
    for i in range(1, nz):
        a_recv(i).wait_recv()
    apply(0)
    apply(1)

    @pl.when(has_prev)
    def _():
        for i in range(2):
            relay(i).wait_recv()

    prev_step(0, xc == 1)
    prev_step(1, xc == 0)
    for t in range(2):
        outs[t * tile:(t + 1) * tile] = result(oc, cnt_pair, t)
        out_send(t).start()
    for t in range(2):
        mixed_ref[t * tile:(t + 1) * tile, mine] = result(xc, cnt_own, t)
    if cells > 1:
        new_swap().start()
        own_ref[xc] = newb[...]
    new_swap().wait_recv()
    own_ref[oc] = xbuf[...]
    for t in range(2):
        out_send(t).wait_recv()
        mixed_ref[t * tile:(t + 1) * tile, other] = outr[t * tile:(t + 1) * tile]

    meta_pair().wait_send()
    for i in range(3):
        swap(i).wait_send()

    @pl.when(has_next)
    def _():
        meta_next(1).wait_send()
        meta_next(0).wait_send()
        for i in range(2):
            direct(i).wait_send()
            relay(i).wait_send()

    for i in range(1, nz):
        z_send(i).wait_send()
        a_send(i).wait_send()
    new_swap().wait_send()
    for t in range(2):
        out_send(t).wait_send()
    if cells > 1:
        @pl.loop(1, cells)
        def _(i):
            cross_send(i).wait_send()


def on_device(n, queries, keys, values, rates, windows, counts, fast):
    tok, width = queries.shape
    fh, heads, mats, dh = fast.shape
    cell = min(n, 8)
    nz = cell // 2
    cells = n // cell
    rows = fh // nz
    count_row = jnp.broadcast_to(counts[:, None].astype(F32), (8 - heads, tok))
    meta = jnp.concatenate([rates, count_row], axis=0)
    fast_t = jnp.transpose(fast, (1, 2, 0, 3))
    vmem = pl.BlockSpec(memory_space=pltpu.VMEM)
    smem = pl.BlockSpec(memory_space=pltpu.SMEM)
    share = (mats, rows // 2, dh) if cells == 1 else (nz, mats, rows, dh)
    dma = pltpu.SemaphoreType.DMA
    near = max(nz - 1, 1)
    mixed, own = pl.pallas_call(
        functools.partial(kernel, n, cell),
        out_shape=(
            jax.ShapeDtypeStruct((tok, width), BF16),
            jax.ShapeDtypeStruct((heads,) + share, BF16),
        ),
        in_specs=[vmem, vmem, vmem, vmem, smem, vmem],
        out_specs=(vmem, vmem),
        scratch_shapes=[
            pltpu.VMEM((3, 2, tok, dh), BF16),
            pltpu.VMEM((2, 2, tok, dh), BF16),
            pltpu.VMEM((3, 8, tok), F32),
            pltpu.VMEM((nz, mats, rows, dh), BF16),
            pltpu.VMEM((nz, mats, rows, dh), F32),
            pltpu.VMEM((near, mats, rows, dh), BF16),
            pltpu.VMEM((cells, mats, rows, dh) if cells > 1 else (1, 1, 16, 128), BF16),
            pltpu.VMEM((nz, mats, rows, dh), BF16),
            pltpu.VMEM(share, BF16),
            pltpu.VMEM((2, tok, dh), F32),
            pltpu.VMEM((2, tok, 1), F32),
            pltpu.VMEM((2, tok, 1), F32),
            pltpu.VMEM((2, tok, dh), F32),
            pltpu.VMEM((tok, dh), BF16),
            pltpu.VMEM((tok, dh), BF16),
            dma((3,)), dma((3,)), dma((2,)), dma((2,)), dma((2,)), dma((2,)),
            dma((3,)), dma((3,)), dma((near,)), dma((near,)),
            dma((max(cells - 1, 1),)), dma((max(cells - 1, 1),)),
            dma((near,)), dma((near,)), dma((1,)), dma((1,)), dma((2,)), dma((2,)),
        ],
        compiler_params=pltpu.CompilerParams(
            collective_id=0, has_side_effects=True, vmem_limit_bytes=50 * 2**20
        ),
    )(queries, keys, values, meta, windows, fast_t)
    if cells == 1:
        new_own = jnp.transpose(own, (2, 0, 1, 3))
    else:
        full = jnp.transpose(own, (1, 3, 0, 2, 4)).reshape(fh, heads, mats, dh)
        part = fh // n
        new_own = lax.dynamic_slice_in_dim(full, lax.axis_index("ctx") * part, part, 0)
    return (mixed, new_own)


def solution(mesh):
    in_specs = (
        P(("groups", "ctx"), "head"),
        P(("groups", "ctx"), "head"),
        P(("groups", "ctx"), "head"),
        P("head", ("groups", "ctx")),
        P(("groups", "head")),
        P(("groups", "ctx")),
        P(None, "head", None, None),
    )
    out_specs = (P(("groups", "ctx"), "head"), P(("groups", "ctx"), "head", None, None))
    return jax.shard_map(
        functools.partial(on_device, mesh.shape["ctx"]),
        mesh=mesh, in_specs=in_specs, out_specs=out_specs, check_vma=False
    )
```

```python
import functools
import jax
import jax.numpy as jnp
from jax import lax
from jax.experimental import pallas as pl
from jax.experimental.pallas import tpu as pltpu
from jax.sharding import PartitionSpec as P

MESH = pl.DeviceIdType.MESH
NT = (((1,), (1,)), ((), ()))
TN = (((0,), (0,)), ((), ()))
F32 = jnp.float32
BF16 = jnp.bfloat16


def dot(a, b, dims=None):
    if dims is None:
        return jnp.dot(a, b, preferred_element_type=F32)
    return lax.dot_general(a, b, dims, preferred_element_type=F32)


def kernel(n, cell, q_ref, k_ref, v_ref, meta_ref, win_ref, fast_ref,
           mixed_ref, own_ref,
           kvq, prev, metas, gs, g32, rz, cross, newb, xbuf, acc, mx, den, ttt, outs, outr,
           x_s, x_r, d_s, d_r, y_s, y_r, m_s, m_r, z_s, z_r, c_s, c_r, a_s, a_r, n_s, n_r, o_s, o_r):
    _, _, fh, dh = fast_ref.shape
    tok = q_ref.shape[0]
    length = tok * n
    me = lax.axis_index("ctx")
    nz = cell // 2
    cells = n // cell
    rows = fh // nz
    half = rows // 2
    base = me // cell * cell
    zc = me % cell // 2
    xc = me % 2
    oc = 1 - xc
    partner = me + 1 - 2 * xc
    tile = tok // 2
    has_prev = me >= 2
    has_next = me + 2 < n

    barrier = pltpu.get_barrier_semaphore()

    @pl.loop(1, n)
    def _(i):
        pl.semaphore_signal(barrier, inc=1, device_id={"ctx": lax.rem(me + i, n)}, device_id_type=MESH)

    pl.semaphore_wait(barrier, n - 1)

    def rdma(src, dst, ssem, rsem, target):
        return pltpu.make_async_remote_copy(
            src_ref=src, dst_ref=dst, send_sem=ssem, recv_sem=rsem,
            device_id={"ctx": target}, device_id_type=MESH)

    refs = (k_ref, v_ref, q_ref)
    mine = pl.ds(pl.multiple_of(xc * dh, dh), dh)
    other = pl.ds(pl.multiple_of(oc * dh, dh), dh)

    def swap(i):
        return rdma(refs[i].at[:, other], kvq.at[i, xc], x_s.at[i], x_r.at[i], partner)

    def direct(i):
        return rdma(refs[i].at[:, mine], prev.at[i, xc], d_s.at[i], d_r.at[i], me + 2)

    def relay(i):
        return rdma(kvq.at[i, oc], prev.at[i, oc], y_s.at[i], y_r.at[i], me + 2)

    def meta_pair():
        return rdma(meta_ref, metas.at[2], m_s.at[0], m_r.at[0], partner)

    def meta_next(same):
        return rdma(meta_ref, metas.at[xc], m_s.at[2 - same], m_r.at[2 - same], (me if same else partner) + 2)

    def near_z(up):
        return me + 2 if up else me - 2

    def sum_send(up, t):
        return rdma(gs.at[t], rz.at[up, t], z_s.at[up, t], z_r.at[up, t], near_z(up))

    def cross_send(i):
        return rdma(cross.at[cells - 1], cross.at[i - 1], c_s.at[i - 1], c_r.at[i - 1], lax.rem(me + i * cell, n))

    def row_send(up, d, block):
        b = newb.at[block]
        return rdma(b, b, a_s.at[up, d], a_r.at[up, d], near_z(up))

    def new_swap():
        if cells == 1:
            part = newb.at[zc, :, pl.ds(pl.multiple_of(oc * half, half), half)]
        else:
            part = newb
        return rdma(part, xbuf, n_s.at[0], n_r.at[0], partner)

    def out_send(t):
        r = pl.ds(t * tile, tile)
        return rdma(outs.at[r], outr.at[r], o_s.at[t], o_r.at[t], partner)

    meta_pair().start()

    @pl.when(has_next)
    def _():
        meta_next(1).start()
        meta_next(0).start()

    for i in range(2):
        swap(i).start()

        @pl.when(has_next)
        def _():
            direct(i).start()

    for i in range(3):
        kvq[i, xc] = refs[i][:, mine]

    window = win_ref[xc]

    def count_of(m):
        return m[2:3, 0:1].astype(jnp.int32)

    def valid_of(cnt):
        return lax.broadcasted_iota(jnp.int32, (tok, 1), 0) < cnt

    cnt_own = count_of(meta_ref)

    def grads(s, meta, first):
        k = kvq[0, s]
        v = kvq[1, s]
        h1 = dot(k, fast_ref[xc, 0], NT)
        dg = dot(v, fast_ref[xc, 1], NT)
        h3 = dot(k, fast_ref[xc, 2], NT)
        turned = jnp.transpose(meta[...])
        rate = jnp.where(xc == 0, turned[:, 0:1], turned[:, 1:2])
        coef = -(rate * valid_of(count_of(meta)).astype(F32))
        sg = jax.nn.sigmoid(h1)
        cs = coef * sg
        cdg = cs * dg
        dh1 = (cdg * h3 * (1.0 + h1 * (1.0 - sg))).astype(BF16)
        dh3 = (cdg * h1).astype(BF16)
        e2 = (cs * h1 * h3).astype(BF16)
        for m, (left, right) in enumerate(((dh1, k), (e2, v), (dh3, k))):
            g = dot(left, right, TN)
            for z in range(nz):
                part = g[z * rows:(z + 1) * rows]
                if first:
                    g32[z, m] = part
                else:
                    part = part + g32[z, m]
                    g32[z, m] = part

    def sum_step(up, t):
        @pl.when(zc < t if up else zc > t)
        def _():
            inner = zc > 0 if up else zc < nz - 1

            @pl.when(inner)
            def _():
                sum_send(up, t).wait_recv()
                gs[t] = (g32[t] + rz[up, t].astype(F32)).astype(BF16)

            @pl.when(jnp.logical_not(inner))
            def _():
                gs[t] = g32[t].astype(BF16)

            sum_send(up, t).start()

    def sums():
        for i in range(nz - 1):
            sum_step(1, nz - 1 - i)
            sum_step(0, i)

    def norm():
        for up in (1, 0):
            @pl.when(zc > 0 if up else zc < nz - 1)
            def _():
                sum_send(up, zc).wait_recv()
                g32[zc] = g32[zc] + rz[up, zc].astype(F32)

        total = g32[zc]
        if cells > 1:
            cross[cells - 1] = total.astype(BF16)
            g32[zc] = total

            @pl.loop(1, cells)
            def _(i):
                cross_send(i).start()

            @pl.loop(1, cells)
            def _(i):
                cross_send(i).wait_recv()
                g32[zc] = g32[zc] + cross[i - 1].astype(F32)

            total = g32[zc]
        old = fast_ref[xc, :, pl.ds(pl.multiple_of(zc * rows, rows), rows), :].astype(F32)
        upd = old - total * length ** (-0.5)
        scale = lax.rsqrt(jnp.mean(upd * upd, axis=-1, keepdims=True) + 1e-06) * dh ** (-0.5)
        newb[zc] = (upd * scale).astype(BF16)
        for up in (1, 0):
            @pl.when(zc < nz - 1 if up else zc > 0)
            def _():
                row_send(up, 0, zc).start()

        if cells == 1:
            new_swap().start()
            own_ref[xc] = newb[zc, :, pl.ds(pl.multiple_of(xc * half, half), half)]

    def gather(d):
        for up in (1, 0):
            block = zc - d if up else zc + d

            @pl.when(block >= 0 if up else block < nz)
            def _():
                row_send(up, d - 1, block).wait_recv()

                @pl.when(zc < nz - 1 if up else zc > 0)
                def _():
                    row_send(up, d, block).start()

    def attend(qs, seg, t, k, v, j0, cnt):
        r = slice(t * tile, (t + 1) * tile)
        nk = k.shape[0]
        sc = dot(kvq[2, qs, r], k, NT) * dh ** (-0.5)
        i = lax.broadcasted_iota(jnp.int32, (tile, nk), 0) + t * tile
        j = lax.broadcasted_iota(jnp.int32, (tile, nk), 1) + j0
        kv = (lax.broadcasted_iota(jnp.int32, (1, nk), 1) + j0) < cnt
        diff = i - j + seg * tok
        if seg == 0:
            ok = ((diff >= 0) & kv) | (diff == 0)
        else:
            ok = (diff < window) & kv
        sc = jnp.where(ok, sc, -1e30)
        top = jnp.max(sc, axis=1, keepdims=True)
        if seg == 0:
            p = jnp.exp(sc - top)
            mx[qs, r] = top
            den[qs, r] = jnp.sum(p, axis=1, keepdims=True)
            acc[qs, r] = dot(p.astype(BF16), v)
        else:
            old = mx[qs, r]
            top = jnp.maximum(old, top)
            p = jnp.exp(sc - top)
            fix = jnp.exp(old - top)
            mx[qs, r] = top
            den[qs, r] = den[qs, r] * fix + jnp.sum(p, axis=1, keepdims=True)
            acc[qs, r] = acc[qs, r] * fix + dot(p.astype(BF16), v)

    def causal(s, cnt):
        attend(s, 0, 0, kvq[0, s, :tile], kvq[1, s, :tile], 0, cnt)
        attend(s, 0, 1, kvq[0, s], kvq[1, s], 0, cnt)

    def full(qs, k, v, cnt):
        for t in range(2):
            attend(qs, 1, t, k, v, 0, cnt)

    def far(qs, ks, cnt):
        attend(qs, 2, 0, prev[0, ks], prev[1, ks], 0, cnt)
        attend(qs, 2, 1, prev[0, ks, tile:], prev[1, ks, tile:], tile, cnt)

    def prev_step(ks, arrived):
        @pl.when(jnp.logical_and(has_prev, arrived))
        def _():
            cnt = count_of(metas[ks])
            far(ks, ks, cnt)
            if ks == 1:
                full(0, prev[0, 1], prev[1, 1], cnt)

    def apply(s):
        w = [newb[:, m].reshape(fh, dh) for m in range(3)]
        for t in range(2):
            r = slice(t * tile, (t + 1) * tile)
            q = kvq[2, s, r]
            a1 = dot(q, w[0], NT)
            a3 = dot(q, w[2], NT)
            ga = (a1 * jax.nn.sigmoid(a1) * a3).astype(BF16)
            ttt[s, r] = dot(ga, w[1]) * fh ** (-0.5)

    def result(s, cnt, t):
        r = slice(t * tile, (t + 1) * tile)
        return jnp.where(valid_of(cnt)[r], acc[s, r] / den[s, r] + ttt[s, r], 0.0).astype(BF16)

    grads(xc, meta_ref, True)
    causal(xc, cnt_own)
    meta_pair().wait_recv()
    cnt_pair = count_of(metas[2])
    for i in range(2):
        swap(i).wait_recv()
    swap(2).start()
    grads(oc, metas.at[2], False)

    @pl.when(has_next)
    def _():
        relay(0).start()

    sums()
    swap(2).wait_recv()
    causal(oc, cnt_pair)
    full(1, kvq[0, 0], kvq[1, 0], jnp.where(xc == 0, cnt_own, cnt_pair))
    norm()

    @pl.when(has_next)
    def _():
        relay(1).start()

    @pl.when(has_prev)
    def _():
        meta_next(1).wait_recv()
        meta_next(0).wait_recv()
        for i in range(2):
            direct(i).wait_recv()

    if nz > 1:
        gather(1)
    prev_step(0, xc == 0)
    prev_step(1, xc == 1)
    for d in range(2, nz):
        gather(d)
    apply(0)
    apply(1)

    @pl.when(has_prev)
    def _():
        for i in range(2):
            relay(i).wait_recv()

    prev_step(0, xc == 1)
    prev_step(1, xc == 0)
    for t in range(2):
        outs[t * tile:(t + 1) * tile] = result(oc, cnt_pair, t)
        out_send(t).start()
    for t in range(2):
        mixed_ref[t * tile:(t + 1) * tile, mine] = result(xc, cnt_own, t)
    if cells > 1:
        new_swap().start()
        own_ref[xc] = newb[...]
    new_swap().wait_recv()
    own_ref[oc] = xbuf[...]
    for t in range(2):
        out_send(t).wait_recv()
        mixed_ref[t * tile:(t + 1) * tile, other] = outr[t * tile:(t + 1) * tile]

    meta_pair().wait_send()
    for i in range(3):
        swap(i).wait_send()

    @pl.when(has_next)
    def _():
        meta_next(1).wait_send()
        meta_next(0).wait_send()
        for i in range(2):
            direct(i).wait_send()
            relay(i).wait_send()

    for up in (1, 0):
        for t in range(nz):
            @pl.when(zc < t if up else zc > t)
            def _():
                sum_send(up, t).wait_send()

        for d in range(nz - 1):
            block = zc - d if up else zc + d

            @pl.when(jnp.logical_and(block >= 0, zc < nz - 1) if up else jnp.logical_and(block < nz, zc > 0))
            def _():
                row_send(up, d, block).wait_send()

    new_swap().wait_send()
    for t in range(2):
        out_send(t).wait_send()
    if cells > 1:
        @pl.loop(1, cells)
        def _(i):
            cross_send(i).wait_send()


def on_device(n, queries, keys, values, rates, windows, counts, fast):
    tok, width = queries.shape
    fh, heads, mats, dh = fast.shape
    cell = min(n, 8)
    nz = cell // 2
    cells = n // cell
    rows = fh // nz
    count_row = jnp.broadcast_to(counts[:, None].astype(F32), (8 - heads, tok))
    meta = jnp.concatenate([rates, count_row], axis=0)
    fast_t = jnp.transpose(fast, (1, 2, 0, 3))
    vmem = pl.BlockSpec(memory_space=pltpu.VMEM)
    smem = pl.BlockSpec(memory_space=pltpu.SMEM)
    share = (mats, rows // 2, dh) if cells == 1 else (nz, mats, rows, dh)
    dma = pltpu.SemaphoreType.DMA
    mixed, own = pl.pallas_call(
        functools.partial(kernel, n, cell),
        out_shape=(
            jax.ShapeDtypeStruct((tok, width), BF16),
            jax.ShapeDtypeStruct((heads,) + share, BF16),
        ),
        in_specs=[vmem, vmem, vmem, vmem, smem, vmem],
        out_specs=(vmem, vmem),
        scratch_shapes=[
            pltpu.VMEM((3, 2, tok, dh), BF16),
            pltpu.VMEM((2, 2, tok, dh), BF16),
            pltpu.VMEM((3, 8, tok), F32),
            pltpu.VMEM((nz, mats, rows, dh), BF16),
            pltpu.VMEM((nz, mats, rows, dh), F32),
            pltpu.VMEM((2, nz, mats, rows, dh), BF16),
            pltpu.VMEM((cells, mats, rows, dh) if cells > 1 else (1, 1, 16, 128), BF16),
            pltpu.VMEM((nz, mats, rows, dh), BF16),
            pltpu.VMEM(share, BF16),
            pltpu.VMEM((2, tok, dh), F32),
            pltpu.VMEM((2, tok, 1), F32),
            pltpu.VMEM((2, tok, 1), F32),
            pltpu.VMEM((2, tok, dh), F32),
            pltpu.VMEM((tok, dh), BF16),
            pltpu.VMEM((tok, dh), BF16),
            dma((3,)), dma((3,)), dma((2,)), dma((2,)), dma((2,)), dma((2,)),
            dma((3,)), dma((3,)), dma((2, nz)), dma((2, nz)),
            dma((max(cells - 1, 1),)), dma((max(cells - 1, 1),)),
            dma((2, nz)), dma((2, nz)), dma((1,)), dma((1,)), dma((2,)), dma((2,)),
        ],
        compiler_params=pltpu.CompilerParams(
            collective_id=0, has_side_effects=True, vmem_limit_bytes=50 * 2**20
        ),
    )(queries, keys, values, meta, windows, fast_t)
    if cells == 1:
        new_own = jnp.transpose(own, (2, 0, 1, 3))
    else:
        full = jnp.transpose(own, (1, 3, 0, 2, 4)).reshape(fh, heads, mats, dh)
        part = fh // n
        new_own = lax.dynamic_slice_in_dim(full, lax.axis_index("ctx") * part, part, 0)
    return (mixed, new_own)


def solution(mesh):
    in_specs = (
        P(("groups", "ctx"), "head"),
        P(("groups", "ctx"), "head"),
        P(("groups", "ctx"), "head"),
        P("head", ("groups", "ctx")),
        P(("groups", "head")),
        P(("groups", "ctx")),
        P(None, "head", None, None),
    )
    out_specs = (P(("groups", "ctx"), "head"), P(("groups", "ctx"), "head", None, None))
    return jax.shard_map(
        functools.partial(on_device, mesh.shape["ctx"]),
        mesh=mesh, in_specs=in_specs, out_specs=out_specs, check_vma=False
    )
```
